256 devices in a mesh: node: 16 (over x, y_lo, core), tm: 16 (over y_hi, z).
Axes of the slice: x: 4, y: 4 (y_hi: 2, y_lo: 2; y = y_hi * 2 + y_lo), z: 8, core: 2. Of those that a mesh axis runs over, the one named last changes fastest.
Arguments:
- series: bfloat16 [48, 4096, 256], P(None, ('node', 'tm')), may hold values from -16 to 16
- t_query: bfloat16 [256, 256], replicated, may hold values from -1 to 1
- t_key: bfloat16 [256, 256], replicated, may hold values from -5 to 5
- t_value: bfloat16 [256, 256], replicated, may hold values from -0.375 to 0.375
- t_out: bfloat16 [256, 256], replicated, may hold values from -0.375 to 0.375
- s_query: bfloat16 [256, 256], replicated, may hold values from -1 to 1
- s_key: bfloat16 [256, 256], replicated, may hold values from -5 to 5
- s_value: bfloat16 [256, 256], replicated, may hold values from -0.375 to 0.375
- s_out: bfloat16 [256, 256], replicated, may hold values from -0.375 to 0.375
- gain_first: float32 [256], replicated, may hold values from 0.25 to 1.75
- gain_second: float32 [256], replicated, may hold values from 0.25 to 1.75
Outputs:
- output: bfloat16 [48, 4096, 256], P(None, ('node', 'tm'))
The draws below stay inside these ranges and needn't reach their ends.
All inputs are finite; a program needn't handle non-finite values.
Results may differ from the reference program's by a relative error of at most 0.0092.
Values may be sent and summed in bfloat16 or wider, within the bound.
A program may use at most 64 MiB of HBM per device.

```python
import math
import jax
import jax.numpy as jnp
from jax import lax

D = 256
HEADS = 8
T_SIZE = 48
NODES = 4096


def shared_base(key, marker):
    folded = jax.random.fold_in(key, marker)
    return jnp.clip(jax.random.normal(folded, (D, D), jnp.float32), -5.0, 5.0) / math.sqrt(D)


def fresh_noise(key):
    return jnp.clip(jax.random.normal(key, (D, D), jnp.float32), -5.0, 5.0) / math.sqrt(D)


def draw_series(key, part):
    key = jax.random.fold_in(key, 5)
    first_key, second_key = jax.random.split(key)
    entries = jnp.clip(jax.random.normal(first_key, (T_SIZE, NODES, D), jnp.float32), -4.0, 4.0)
    scales = jnp.exp(jax.random.uniform(second_key, (D,), jnp.float32, 0.0, math.log(4.0)))
    return (entries * scales).astype(jnp.bfloat16)


def draw_t_query(key, part):
    return jnp.clip(1.5 * shared_base(key, 11), -1.0, 1.0).astype(jnp.bfloat16)


def draw_t_key(key, part):
    key = jax.random.fold_in(key, 3)
    noise = fresh_noise(key)
    result = noise
    return jnp.clip(result, -5.0, 5.0).astype(jnp.bfloat16)


def draw_s_query(key, part):
    return jnp.clip(2.5 * shared_base(key, 12), -1.0, 1.0).astype(jnp.bfloat16)


def draw_s_key(key, part):
    key = jax.random.fold_in(key, 4)
    noise = fresh_noise(key)
    result = noise
    return jnp.clip(result, -5.0, 5.0).astype(jnp.bfloat16)


def centred(stream_key, dims, scale, limit, held_as=jnp.bfloat16):
    values = jax.random.normal(stream_key, dims, jnp.float32) * scale
    return jnp.minimum(jnp.maximum(values, -limit), limit).astype(held_as)


def setup_inputs(seed: int = 0) -> dict:
    splits = jax.random.split(jax.random.key(seed), 12)
    series = draw_series(jax.random.fold_in(splits[11], 71), 0)
    t_query = draw_t_query(jax.random.fold_in(splits[11], 71), 0)
    t_key = draw_t_key(jax.random.fold_in(splits[11], 71), 0)
    t_value = centred(splits[3], (D, D), D ** -0.5, 0.375)
    t_out = centred(splits[4], (D, D), D ** -0.5, 0.375)
    s_query = draw_s_query(jax.random.fold_in(splits[11], 71), 0)
    s_key = draw_s_key(jax.random.fold_in(splits[11], 71), 0)
    s_value = centred(splits[7], (D, D), D ** -0.5, 0.375)
    s_out = centred(splits[8], (D, D), D ** -0.5, 0.375)
    gain_first = jnp.clip(1.0 + 0.15 * jax.random.normal(splits[9], (D,), jnp.float32), 0.25, 1.75)
    gain_second = jnp.clip(1.0 + 0.15 * jax.random.normal(splits[10], (D,), jnp.float32), 0.25, 1.75)
    return dict(series=series, t_query=t_query, t_key=t_key, t_value=t_value, t_out=t_out, s_query=s_query, s_key=s_key, s_value=s_value, s_out=s_out, gain_first=gain_first, gain_second=gain_second)


def layer_norm(values, gain):
    center = values - lax.optimization_barrier(jnp.mean(values, axis=-1, keepdims=True))
    spread = lax.optimization_barrier(jnp.mean(center * center, axis=-1, keepdims=True))
    return center * lax.rsqrt(spread + 1e-05) * gain

def linear(values, weight):
    flattened = values.reshape(-1, values.shape[-1])
    result = jnp.dot(flattened, weight, preferred_element_type=jnp.float32)
    return result.reshape(values.shape[:-1] + (weight.shape[1],))

def temporal_part(series, t_query, t_key, t_value, t_out):
    step_count, node_count, model_width = series.shape
    head_dim = model_width // HEADS
    shaped = (step_count, node_count, HEADS, head_dim)
    queries = linear(series, t_query).astype(jnp.bfloat16).reshape(shaped)
    key_rows = linear(series, t_key).astype(jnp.bfloat16).reshape(shaped)
    value_rows = linear(series, t_value).astype(jnp.bfloat16).reshape(shaped)
    scores = jnp.einsum('snhe,tnhe->nhst', queries.astype(jnp.float32), key_rows.astype(jnp.float32)) * (1.0 / math.sqrt(head_dim))
    causal = lax.broadcasted_iota(jnp.int32, (step_count, step_count), 0) >= lax.broadcasted_iota(jnp.int32, (step_count, step_count), 1)
    scores = jnp.where(causal, scores, -jnp.inf)
    row_max = lax.optimization_barrier(jnp.max(scores, axis=-1, keepdims=True))
    weights_exp = jnp.exp(scores - row_max)
    total = lax.optimization_barrier(jnp.sum(weights_exp, axis=-1))
    rounded = lax.optimization_barrier(weights_exp.astype(jnp.bfloat16)).astype(jnp.float32)
    mixed_heads = jnp.einsum('nhst,tnhe->snhe', rounded, value_rows.astype(jnp.float32))
    mixed_heads = mixed_heads / jnp.transpose(total, (2, 0, 1))[..., None]
    mixed_heads = mixed_heads.astype(jnp.bfloat16).reshape(step_count, node_count, model_width)
    return series.astype(jnp.float32) + linear(mixed_heads, t_out)

def spatial_one(triple):
    queries, key_rows, value_rows = triple
    scale = 1.0 / math.sqrt(queries.shape[-1])
    scores = jnp.dot(queries, key_rows.T, preferred_element_type=jnp.float32) * scale
    row_max = lax.optimization_barrier(jnp.max(scores, axis=-1, keepdims=True))
    weights_exp = jnp.exp(scores - row_max)
    total = lax.optimization_barrier(jnp.sum(weights_exp, axis=-1, keepdims=True))
    summed = jnp.dot(weights_exp.astype(jnp.bfloat16), value_rows, preferred_element_type=jnp.float32)
    return (summed / total).astype(jnp.bfloat16)

def reference(series, t_query, t_key, t_value, t_out, s_query, s_key, s_value, s_out, gain_first, gain_second):
    step_count, node_count, model_width = series.shape
    head_dim = model_width // HEADS
    first = temporal_part(series, t_query, t_key, t_value, t_out)
    hidden = layer_norm(first, gain_first).astype(jnp.bfloat16)

    def by_head(weight):
        projected = linear(hidden, weight).astype(jnp.bfloat16)
        projected = projected.reshape(step_count, node_count, HEADS, head_dim)
        return jnp.transpose(projected, (0, 2, 1, 3)).reshape(step_count * HEADS, node_count, head_dim)
    mixed_heads = lax.map(spatial_one, (by_head(s_query), by_head(s_key), by_head(s_value)))
    mixed_heads = mixed_heads.reshape(step_count, HEADS, node_count, head_dim)
    mixed_heads = jnp.transpose(mixed_heads, (0, 2, 1, 3)).reshape(step_count, node_count, model_width)
    second = hidden.astype(jnp.float32) + linear(mixed_heads, s_out)
    return layer_norm(second, gain_second).astype(jnp.bfloat16)
```

```python
import functools
import math

import jax
import jax.numpy as jnp
from jax import lax
from jax.experimental import pallas as pl
from jax.experimental.pallas import tpu as pltpu
from jax.sharding import PartitionSpec as P

HEADS = 8
epsilon = 1e-05
f32, bf16 = jnp.float32, jnp.bfloat16
MESH = pl.DeviceIdType.MESH


def layer_norm(values, gain):
    center = values - jnp.mean(values, axis=-1, keepdims=True)
    spread = jnp.mean(center * center, axis=-1, keepdims=True)
    return center * lax.rsqrt(spread + epsilon) * gain


def linear(values, weight):
    flattened = values.reshape(-1, values.shape[-1])
    result = jnp.dot(flattened, weight, preferred_element_type=f32)
    return result.reshape(values.shape[:-1] + (weight.shape[1],))


def temporal_part(series, t_query, t_key, t_value, t_out):
    step_count, node_count, model_width = series.shape
    head_dim = model_width // HEADS
    shaped = (step_count, node_count, HEADS, head_dim)
    queries = linear(series, t_query).astype(bf16).reshape(shaped)
    key_rows = linear(series, t_key).astype(bf16).reshape(shaped)
    value_rows = linear(series, t_value).astype(bf16).reshape(shaped)
    scores = jnp.einsum(
        "snhe,tnhe->nhst", queries, key_rows, preferred_element_type=f32
    ) * (1.0 / math.sqrt(head_dim))
    causal = lax.broadcasted_iota(jnp.int32, (step_count, step_count), 0) >= lax.broadcasted_iota(
        jnp.int32, (step_count, step_count), 1
    )
    scores = jnp.where(causal, scores, -jnp.inf)
    row_max = jnp.max(scores, axis=-1, keepdims=True)
    weights_exp = jnp.exp(scores - row_max)
    total = jnp.sum(weights_exp, axis=-1)
    mixed_heads = jnp.einsum(
        "nhst,tnhe->snhe", weights_exp.astype(bf16), value_rows, preferred_element_type=f32
    )
    mixed_heads = mixed_heads / jnp.transpose(total, (2, 0, 1))[..., None]
    mixed_heads = mixed_heads.astype(bf16).reshape(step_count, node_count, model_width)
    return series.astype(f32) + linear(mixed_heads, t_out)


def dot_t(a, b):
    return lax.dot_general(a, b, (((1,), (1,)), ((), ())), preferred_element_type=f32)


def dot(a, b):
    return jnp.dot(a, b, preferred_element_type=f32)


def spatial_kernel(
    hid, wq, wk, wv, wo, gain, out,
    keys_in, k_buf, v_buf, q_mask, acc, row_max, result,
    a_send, a_recv, n_send, n_recv, s_send, s_recv, r_send, r_recv,
):
    steps, rows, width = keys_in.shape
    node = lax.axis_index("node")
    me = lax.axis_index("tm")
    groups = 16
    block = rows // 16
    slab = block // groups
    core = node % 2
    y_lo = (node // 2) % 2
    x = node // 4
    sibling = node + 1 - 2 * core
    y_peer = node + 2 - 4 * y_lo
    right = ((x + 1) % 4) * 4 + node % 4
    left = ((x + 3) % 4) * 4 + node % 4
    head_dim = width // HEADS

    barrier = pltpu.get_barrier_semaphore()
    for other in (sibling, y_peer, right, left):
        pl.semaphore_signal(barrier, inc=1, device_id={"node": other}, device_id_type=MESH)

    def greet(k, carry):
        pl.semaphore_signal(
            barrier, inc=1, device_id={"tm": (me + k) % groups}, device_id_type=MESH
        )
        return carry

    lax.fori_loop(1, groups, greet, 0)
    pl.semaphore_wait(barrier, groups - 1 + 4)

    def scatter_copy(t, j):
        return pltpu.make_async_remote_copy(
            src_ref=hid.at[steps * j + t],
            dst_ref=keys_in.at[t, pl.ds(pl.multiple_of(me * slab, slab), slab), :],
            send_sem=a_send.at[t],
            recv_sem=a_recv.at[t],
            device_id={"tm": j},
            device_id_type=MESH,
        )

    for t in range(steps):
        def scatter(k, carry):
            scatter_copy(t, (me + k) % groups).start()
            return carry

        lax.fori_loop(1, groups, scatter, 0)
    for t in range(steps):
        keys_in[t, pl.ds(pl.multiple_of(me * slab, slab), slab), :] = hid[steps * me + t]

    def wait_bytes(ref, sem):
        pltpu.make_async_copy(ref, ref, sem).wait()

    def send(t, src, dst, count, index, other):
        return pltpu.make_async_remote_copy(
            src_ref=keys_in.at[t, pl.ds(src * block, count * block), :],
            dst_ref=keys_in.at[t, pl.ds(dst * block, count * block), :],
            send_sem=n_send.at[t, index],
            recv_sem=n_recv.at[t, index],
            device_id={"node": other},
            device_id_type=MESH,
        )

    def to_sibling(t, src, count, index):
        return pltpu.make_async_remote_copy(
            src_ref=keys_in.at[t, pl.ds(src * block, count * block), :],
            dst_ref=keys_in.at[t, pl.ds((src + 2) * block, count * block), :],
            send_sem=s_send.at[t, index],
            recv_sem=s_recv.at[t, index],
            device_id={"node": sibling},
            device_id_type=MESH,
        )

    def copies(t):
        return [
            send(t, 0, 1, 1, 0, y_peer),
            send(t, 0, 4, 1, 1, right),
            send(t, 0, 8, 1, 2, left),
            send(t, 1, 5, 1, 3, right),
            send(t, 1, 9, 1, 4, left),
            send(t, 4, 12, 1, 5, right),
            send(t, 9, 13, 1, 6, left),
        ]

    def sib_copies(t):
        return [
            to_sibling(t, 0, 1, 0),
            to_sibling(t, 1, 1, 1),
            to_sibling(t, 4, 2, 2),
            to_sibling(t, 8, 2, 3),
            to_sibling(t, 12, 2, 4),
        ]

    def own_ready(t):
        wait_bytes(keys_in.at[t, pl.ds(0, block - slab), :], a_recv.at[t])
        c, s = copies(t), sib_copies(t)
        c[0].start()
        s[0].start()
        c[1].start()
        c[2].start()

    def y_ready(t):
        c, s = copies(t), sib_copies(t)
        c[0].wait_recv()
        s[1].start()
        c[3].start()
        c[4].start()

    def sides_ready(t):
        c, s = copies(t), sib_copies(t)
        c[1].wait_recv()
        c[3].wait_recv()
        c[2].wait_recv()
        c[4].wait_recv()
        c[5].start()
        c[6].start()
        s[2].start()
        s[3].start()

    def opposite_ready(t):
        c, s = copies(t), sib_copies(t)
        c[5].wait_recv()
        c[6].wait_recv()
        s[4].start()

    own_ready(0)
    chunk = 4 * block
    v_buf[:, :, width // 2:] = jnp.ones((2, chunk, width // 2), bf16)
    scale = math.log2(math.e) / math.sqrt(head_dim)
    y_ready(0)

    def tick(g, carry):
        t = g // 8
        u = g % 8
        part = u // 2
        half = u % 2

        @pl.when(u == 0)
        def _():
            own = keys_in[t, pl.ds(0, block), :]
            q = (dot(own, wq[...]) * scale).astype(bf16)
            lane = lax.broadcasted_iota(jnp.int32, (block, width), 1) // head_dim
            for h in range(HEADS):
                q_mask[h] = jnp.where(lane == h, q, jnp.zeros_like(q))
            acc[...] = jnp.zeros_like(acc)
            row_max[...] = jnp.full_like(row_max, -1e30)
            s = sib_copies(t)
            s[0].wait_recv()
            s[1].wait_recv()

        @pl.when(u == 1)
        def _():
            sides_ready(t)

        @pl.when(u == 2)
        def _():
            sib_copies(t)[2].wait_recv()

        @pl.when((u == 3) & (t < steps - 1))
        def _():
            own_ready(t + 1)

        @pl.when(u == 4)
        def _():
            sib_copies(t)[3].wait_recv()

        @pl.when(u == 5)
        def _():
            opposite_ready(t)

        @pl.when((u == 5) & (t < steps - 1))
        def _():
            y_ready(t + 1)

        @pl.when(u == 6)
        def _():
            sib_copies(t)[4].wait_recv()

        @pl.when(half == 0)
        def _():
            rows_in = keys_in[t, pl.ds(pl.multiple_of(part * chunk, chunk), chunk), :]
            k_buf[...] = dot(rows_in, wk[...]).astype(bf16)
            v = dot(rows_in, wv[...]).astype(bf16)
            v_buf[0, :, : width // 2] = v[:, : width // 2]
            v_buf[1, :, : width // 2] = v[:, width // 2 :]

        for i in range(HEADS // 2):
            h = half * (HEADS // 2) + i
            s = dot_t(q_mask[h], k_buf[...])
            old = row_max[h]
            new = jnp.maximum(old, jnp.max(s, axis=1, keepdims=True))
            p = jnp.exp2(s - new[:, 0:1]).astype(bf16)
            fade = jnp.exp2(old - new)
            acc[h] = acc[h] * fade[:, 0:1] + dot(p, v_buf[half])
            row_max[h] = new

        @pl.when(u == 7)
        def _():
            lane = lax.broadcasted_iota(jnp.int32, (block, width // 2), 1) // head_dim
            sides = []
            for s in range(2):
                mixed = jnp.zeros((block, width // 2), f32)
                for i in range(HEADS // 2):
                    a = acc[s * (HEADS // 2) + i]
                    mixed = jnp.where(lane == i, a[:, : width // 2] / a[:, width // 2 :], mixed)
                sides.append(mixed.astype(bf16))
            mixed = jnp.concatenate(sides, axis=1)
            own = keys_in[t, pl.ds(0, block), :].astype(f32)
            second = own + dot(mixed, wo[...])
            result[t] = layer_norm(second, gain[...]).astype(bf16)

            def give(k, carry):
                give_copy(t, (me + k) % groups).start()
                return carry

            lax.fori_loop(1, groups, give, 0)

        return carry

    def give_copy(t, j):
        return pltpu.make_async_remote_copy(
            src_ref=result.at[t, pl.ds(pl.multiple_of(j * slab, slab), slab), :],
            dst_ref=out.at[steps * me + t],
            send_sem=r_send.at[t],
            recv_sem=r_recv.at[t],
            device_id={"tm": j},
            device_id_type=MESH,
        )

    lax.fori_loop(0, 8 * steps, tick, 0)

    for t in range(steps):
        out[steps * me + t] = result[t, pl.ds(pl.multiple_of(me * slab, slab), slab), :]
    for t in range(steps):
        wait_bytes(keys_in.at[t, pl.ds(0, block - slab), :], a_send.at[t])
        for c in copies(t) + sib_copies(t):
            c.wait_send()
        wait_bytes(result.at[t, pl.ds(0, block - slab), :], r_send.at[t])
        wait_bytes(result.at[t, pl.ds(0, block - slab), :], r_recv.at[t])


def spatial(hidden, s_query, s_key, s_value, s_out, gain):
    total_steps, nodes, width = hidden.shape
    steps = total_steps // 16
    block = nodes * 16
    chunk = 4 * block
    vmem = pl.BlockSpec(memory_space=pltpu.VMEM)
    return pl.pallas_call(
        spatial_kernel,
        out_shape=jax.ShapeDtypeStruct(hidden.shape, bf16),
        in_specs=[vmem] * 6,
        out_specs=vmem,
        scratch_shapes=[
            pltpu.VMEM((steps, 16 * block, width), bf16),
            pltpu.VMEM((chunk, width), bf16),
            pltpu.VMEM((2, chunk, width), bf16),
            pltpu.VMEM((HEADS, block, width), bf16),
            pltpu.VMEM((HEADS, block, width), f32),
            pltpu.VMEM((HEADS, block, 128), f32),
            pltpu.VMEM((steps, block, width), bf16),
            pltpu.SemaphoreType.DMA((steps,)),
            pltpu.SemaphoreType.DMA((steps,)),
            pltpu.SemaphoreType.DMA((steps, 7)),
            pltpu.SemaphoreType.DMA((steps, 7)),
            pltpu.SemaphoreType.DMA((steps, 5)),
            pltpu.SemaphoreType.DMA((steps, 5)),
            pltpu.SemaphoreType.DMA((steps,)),
            pltpu.SemaphoreType.DMA((steps,)),
        ],
        compiler_params=pltpu.CompilerParams(
            collective_id=0, has_side_effects=True, vmem_limit_bytes=48 * 2**20
        ),
    )(hidden, s_query, s_key, s_value, s_out, gain.reshape(1, width))


def shards(
    series, t_query, t_key, t_value, t_out, s_query, s_key, s_value, s_out, gain_first, gain_second
):
    first = temporal_part(series, t_query, t_key, t_value, t_out)
    hidden = layer_norm(first, gain_first).astype(bf16)
    return spatial(hidden, s_query, s_key, s_value, s_out, gain_second)


def solution(mesh):
    in_specs = (P(None, ("node", "tm"), None), P(), P(), P(), P(), P(), P(), P(), P(), P(), P())
    out_specs = P(None, ("node", "tm"), None)
    return jax.shard_map(shards, mesh=mesh, in_specs=in_specs, out_specs=out_specs, check_vma=False)
```

```python
import math

import jax
import jax.numpy as jnp
from jax import lax
from jax.experimental import pallas as pl
from jax.experimental.pallas import tpu as pltpu
from jax.sharding import PartitionSpec as P

HEADS = 8
epsilon = 1e-05
f32, bf16 = jnp.float32, jnp.bfloat16
MESH = pl.DeviceIdType.MESH
GROUPS = 16
BLOCK_SLOTS = 16


def layer_norm(values, gain):
    center = values - jnp.mean(values, axis=-1, keepdims=True)
    spread = jnp.mean(center * center, axis=-1, keepdims=True)
    return center * lax.rsqrt(spread + epsilon) * gain


def dot_t(a, b):
    return lax.dot_general(a, b, (((1,), (1,)), ((), ())), preferred_element_type=f32)


def dot(a, b):
    return jnp.dot(a, b, preferred_element_type=f32)


def wide(column, count):
    return jnp.concatenate([column] * count, axis=1)


def block_kernel(
    series, tq, tk, tv, to, wq, wk, wv, wo, gain_first, gain_second, out,
    flat_q, flat_k, flat_v, flat_mix, hid,
    keys_in, k_buf, v_buf, q_mask, acc, row_max, result,
    a_send, a_recv, n_send, n_recv, s_send, s_recv, r_send, r_recv,
):
    steps, rows, width = keys_in.shape
    window, slab, _ = series.shape
    block = rows // BLOCK_SLOTS
    half = width // 2
    head_dim = width // HEADS
    scale = math.log2(math.e) / math.sqrt(head_dim)
    node = lax.axis_index("node")
    me = lax.axis_index("tm")
    core = node % 2
    y_lo = (node // 2) % 2
    x = node // 4
    sibling = node + 1 - 2 * core
    y_peer = node + 2 - 4 * y_lo
    right = ((x + 1) % 4) * 4 + node % 4
    left = ((x + 3) % 4) * 4 + node % 4

    barrier = pltpu.get_barrier_semaphore()
    for other in (sibling, y_peer, right, left):
        pl.semaphore_signal(barrier, inc=1, device_id={"node": other}, device_id_type=MESH)

    def greet(k, carry):
        pl.semaphore_signal(
            barrier, inc=1, device_id={"tm": (me + k) % GROUPS}, device_id_type=MESH
        )
        return carry

    lax.fori_loop(1, GROUPS, greet, 0)

    flat = series[...].reshape(window * slab, width)
    for s in range(2):
        cut = pl.ds(s * half, half)
        flat_q[s] = (dot(flat, tq[:, cut]) * scale).astype(bf16).astype(f32)
        flat_k[s] = dot(flat, tk[:, cut]).astype(bf16).astype(f32)
        flat_v[s] = dot(flat, tv[:, cut]).astype(bf16).astype(f32)
    per = 4
    span = per * window
    row_id = lax.broadcasted_iota(jnp.int32, (span, span), 0)
    col_id = lax.broadcasted_iota(jnp.int32, (span, span), 1)

    def owner(index):
        total = jnp.zeros_like(index)
        for k in range(1, per):
            total = total + (index >= k * window).astype(jnp.int32)
        return total

    seen = (row_id >= col_id) & (owner(row_id) == owner(col_id))
    lane = lax.broadcasted_iota(jnp.int32, (span, width), 1) // head_dim
    half_lane = lax.broadcasted_iota(jnp.int32, (span, half), 1) // head_dim
    ones = jnp.ones((span, half), bf16)
    for g in range(slab // per):
        def gather(ref):
            sides = []
            for s in range(2):
                parts = [
                    ref[s, pl.ds(g * per + i, window, stride=slab), :].astype(bf16)
                    for i in range(per)
                ]
                sides.append(jnp.concatenate(parts, axis=0))
            return jnp.concatenate(sides, axis=1)

        q, k, v = gather(flat_q), gather(flat_k), gather(flat_v)
        for s in range(2):
            values = jnp.concatenate([v[:, s * half : (s + 1) * half], ones], axis=1)
            mixed = jnp.zeros((span, half), f32)
            for i in range(HEADS // 2):
                h = s * (HEADS // 2) + i
                scores = dot_t(jnp.where(lane == h, q, jnp.zeros_like(q)), k)
                scores = jnp.where(seen, scores, -1e30)
                top = jnp.max(scores, axis=1, keepdims=True)
                p = jnp.exp2(scores - top).astype(bf16)
                a = dot(p, values)
                mixed = jnp.where(half_lane == i, a[:, :half] / a[:, half:], mixed)
            for i in range(per):
                flat_mix[s, pl.ds(g * per + i, window, stride=slab), :] = mixed[
                    i * window : (i + 1) * window
                ]
    mixed = jnp.concatenate([flat_mix[0].astype(bf16), flat_mix[1].astype(bf16)], axis=1)
    first = flat.astype(f32) + dot(mixed, to[...])
    hid[...] = layer_norm(first, gain_first[...]).astype(bf16).reshape(window, slab, width)

    pl.semaphore_wait(barrier, GROUPS - 1 + 4)

    my_rows = pl.ds(pl.multiple_of(me * slab, slab), slab)

    def scatter(t):
        def one(k, carry):
            j = (me + k) % GROUPS
            pltpu.make_async_remote_copy(
                src_ref=hid.at[steps * j + t],
                dst_ref=keys_in.at[t, my_rows, :],
                send_sem=a_send.at[t],
                recv_sem=a_recv.at[t],
                device_id={"tm": j},
                device_id_type=MESH,
            ).start()
            return carry

        lax.fori_loop(1, GROUPS, one, 0)

    for t in range(steps):
        scatter(t)
    for t in range(steps):
        keys_in[t, my_rows, :] = hid[steps * me + t]

    def wait_bytes(ref, sem):
        pltpu.make_async_copy(ref, ref, sem).wait()

    routes = [
        (0, 2, y_peer),
        (0, 3, right),
        (0, 4, left),
        (2, 8, right),
        (2, 9, left),
        (3, 10, right),
        (9, 11, left),
    ]
    shares = [(0, 1, 1), (2, 5, 3), (8, 12, 2), (10, 14, 2)]

    def route(t, i):
        src, dst, other = routes[i]
        return pltpu.make_async_remote_copy(
            src_ref=keys_in.at[t, pl.ds(src * block, block), :],
            dst_ref=keys_in.at[t, pl.ds(dst * block, block), :],
            send_sem=n_send.at[t, i],
            recv_sem=n_recv.at[t, i],
            device_id={"node": other},
            device_id_type=MESH,
        )

    def share(t, i):
        src, dst, count = shares[i]
        return pltpu.make_async_remote_copy(
            src_ref=keys_in.at[t, pl.ds(src * block, count * block), :],
            dst_ref=keys_in.at[t, pl.ds(dst * block, count * block), :],
            send_sem=s_send.at[t, i],
            recv_sem=s_recv.at[t, i],
            device_id={"node": sibling},
            device_id_type=MESH,
        )

    def own_ready(t):
        wait_bytes(keys_in.at[t, pl.ds(0, block - slab), :], a_recv.at[t])
        share(t, 0).start()
        for i in (0, 1, 2):
            route(t, i).start()

    def near_ready(t):
        for i in (0, 1, 2):
            route(t, i).wait_recv()
        for i in (3, 4, 5):
            route(t, i).start()
        share(t, 1).start()

    def side_ready(t):
        for i in (3, 4):
            route(t, i).wait_recv()
        route(t, 6).start()
        share(t, 2).start()

    def far_ready(t):
        for i in (5, 6):
            route(t, i).wait_recv()
        share(t, 3).start()

    def shared(t, i):
        share(t, i).wait_recv()

    chunk = k_buf.shape[1]
    v_buf[:, :, :, half:] = jnp.ones((2, 2, chunk, half), bf16)
    turn = [0]

    def project_queries(t):
        q = (dot(keys_in[t, pl.ds(0, block), :], wq[...]) * scale).astype(bf16)
        lane = lax.broadcasted_iota(jnp.int32, (block, width), 1) // head_dim
        for h in range(HEADS):
            q_mask[t % 2, h] = jnp.where(lane == h, q, jnp.zeros_like(q))

    def attend(t, parts, fresh):
        slot = turn[0] % 2
        turn[0] += 1
        n = 0
        for start, count in parts:
            rows_in = keys_in[t, pl.ds(start * block, count * block), :]
            here = pl.ds(n, count * block)
            k_buf[slot, here, :] = dot(rows_in, wk[...]).astype(bf16)
            v = dot(rows_in, wv[...]).astype(bf16)
            v_buf[slot, 0, here, :half] = v[:, :half]
            v_buf[slot, 1, here, :half] = v[:, half:]
            n += count * block
        for h in range(HEADS):
            s = dot_t(q_mask[t % 2, h], k_buf[slot, :n, :])
            top = jnp.max(s, axis=1, keepdims=True)
            if fresh:
                new = jnp.broadcast_to(top, (block, 128))
            else:
                old = row_max[t % 2, h]
                new = jnp.maximum(old, top)
            p = jnp.exp2(s - wide(new, n // 128)).astype(bf16)
            update = dot(p, v_buf[slot, h // 4, :n, :])
            if fresh:
                acc[t % 2, h] = update
            else:
                fade = jnp.exp2(old - new)
                acc[t % 2, h] = acc[t % 2, h] * wide(fade, width // 128) + update
            row_max[t % 2, h] = new

    def finish(t):
        lane = lax.broadcasted_iota(jnp.int32, (block, half), 1) // head_dim
        sides = []
        for s in range(2):
            mixed = jnp.zeros((block, half), f32)
            for i in range(HEADS // 2):
                a = acc[t % 2, s * (HEADS // 2) + i]
                mixed = jnp.where(lane == i, a[:, :half] / a[:, half:], mixed)
            sides.append(mixed.astype(bf16))
        mixed = jnp.concatenate(sides, axis=1)
        second = keys_in[t, pl.ds(0, block), :].astype(f32) + dot(mixed, wo[...])
        result[t] = layer_norm(second, gain_second[...]).astype(bf16)

    def give(t):
        def one(k, carry):
            j = (me + k) % GROUPS
            pltpu.make_async_remote_copy(
                src_ref=result.at[t, pl.ds(pl.multiple_of(j * slab, slab), slab), :],
                dst_ref=out.at[steps * me + t],
                send_sem=r_send.at[t],
                recv_sem=r_recv.at[t],
                device_id={"tm": j},
                device_id_type=MESH,
            ).start()
            return carry

        lax.fori_loop(1, GROUPS, one, 0)

    own_ready(0)
    project_queries(0)
    shared(0, 0)
    attend(0, [(0, 2)], True)
    near_ready(0)
    attend(0, [(2, 3)], False)
    shared(0, 1)
    side_ready(0)
    own_ready(1)
    attend(0, [(5, 3)], False)
    shared(0, 2)
    far_ready(0)
    attend(0, [(8, 2), (12, 2)], False)
    shared(0, 3)
    near_ready(1)
    attend(0, [(10, 2), (14, 2)], False)

    shared(1, 0)
    shared(1, 1)
    side_ready(1)
    own_ready(2)
    finish(0)
    project_queries(1)
    attend(1, [(0, 4)], True)
    attend(1, [(4, 4)], False)
    give(0)
    far_ready(1)
    near_ready(2)
    attend(1, [(8, 4)], False)
    shared(1, 2)
    shared(1, 3)
    side_ready(2)
    attend(1, [(12, 4)], False)

    shared(2, 0)
    shared(2, 1)
    far_ready(2)
    finish(1)
    project_queries(2)
    attend(2, [(0, 4)], True)
    attend(2, [(4, 4)], False)
    give(1)
    shared(2, 2)
    shared(2, 3)
    attend(2, [(8, 4)], False)
    attend(2, [(12, 4)], False)
    finish(2)
    give(2)

    for t in range(steps):
        out[steps * me + t] = result[t, my_rows, :]
    for t in range(steps):
        wait_bytes(keys_in.at[t, pl.ds(0, block - slab), :], a_send.at[t])
        for i in range(len(routes)):
            route(t, i).wait_send()
        for i in range(len(shares)):
            share(t, i).wait_send()
        wait_bytes(result.at[t, pl.ds(0, block - slab), :], r_send.at[t])
        wait_bytes(result.at[t, pl.ds(0, block - slab), :], r_recv.at[t])


def shards(
    series, t_query, t_key, t_value, t_out, s_query, s_key, s_value, s_out, gain_first, gain_second
):
    window, slab, width = series.shape
    steps = window // GROUPS
    block = slab * GROUPS
    chunk = 4 * block
    vmem = pl.BlockSpec(memory_space=pltpu.VMEM)
    flat = pltpu.VMEM((2, window * slab, width // 2), f32)
    return pl.pallas_call(
        block_kernel,
        out_shape=jax.ShapeDtypeStruct(series.shape, bf16),
        in_specs=[vmem] * 11,
        out_specs=vmem,
        scratch_shapes=[
            flat,
            flat,
            flat,
            flat,
            pltpu.VMEM((window, slab, width), bf16),
            pltpu.VMEM((steps, BLOCK_SLOTS * block, width), bf16),
            pltpu.VMEM((2, chunk, width), bf16),
            pltpu.VMEM((2, 2, chunk, width), bf16),
            pltpu.VMEM((2, HEADS, block, width), bf16),
            pltpu.VMEM((2, HEADS, block, width), f32),
            pltpu.VMEM((2, HEADS, block, 128), f32),
            pltpu.VMEM((steps, block, width), bf16),
            pltpu.SemaphoreType.DMA((steps,)),
            pltpu.SemaphoreType.DMA((steps,)),
            pltpu.SemaphoreType.DMA((steps, 7)),
            pltpu.SemaphoreType.DMA((steps, 7)),
            pltpu.SemaphoreType.DMA((steps, 4)),
            pltpu.SemaphoreType.DMA((steps, 4)),
            pltpu.SemaphoreType.DMA((steps,)),
            pltpu.SemaphoreType.DMA((steps,)),
        ],
        compiler_params=pltpu.CompilerParams(
            collective_id=0, has_side_effects=True, vmem_limit_bytes=48 * 2**20
        ),
    )(
        series, t_query, t_key, t_value, t_out, s_query, s_key, s_value, s_out,
        gain_first.reshape(1, width), gain_second.reshape(1, width),
    )


def solution(mesh):
    in_specs = (P(None, ("node", "tm"), None), P(), P(), P(), P(), P(), P(), P(), P(), P(), P())
    out_specs = P(None, ("node", "tm"), None)
    return jax.shard_map(shards, mesh=mesh, in_specs=in_specs, out_specs=out_specs, check_vma=False)
```

```python
import math

import jax
import jax.numpy as jnp
from jax import lax
from jax.experimental import pallas as pl
from jax.experimental.pallas import tpu as pltpu
from jax.sharding import PartitionSpec as P

HEADS = 8
epsilon = 1e-05
f32, bf16 = jnp.float32, jnp.bfloat16
MESH = pl.DeviceIdType.MESH
GROUPS = 16
BLOCK_SLOTS = 16


def layer_norm(values, gain):
    center = values - jnp.mean(values, axis=-1, keepdims=True)
    spread = jnp.mean(center * center, axis=-1, keepdims=True)
    return center * lax.rsqrt(spread + epsilon) * gain


def dot_t(a, b):
    return lax.dot_general(a, b, (((1,), (1,)), ((), ())), preferred_element_type=f32)


def dot(a, b):
    return jnp.dot(a, b, preferred_element_type=f32)


def wide(column, count):
    return jnp.concatenate([column] * count, axis=1)


def block_kernel(
    *refs,
):
    operands, refs = refs[:11], refs[11:]
    staged, refs = refs[1:12], (refs[0],) + refs[12:]
    body(operands, staged, *refs)


def body(
    operands, staged, out, load_sem, keep_sem,
    flat_q, flat_k, flat_v, flat_mix, hid,
    keys_in, k_buf, v_buf, q_mask, acc, row_max, result,
    a_send, a_recv, n_send, n_recv, s_send, s_recv, r_send, r_recv,
):
    series, tq, tk, tv, to, wq, wk, wv, wo, gain_first, gain_second = staged
    steps, rows, width = keys_in.shape
    window, slab, _ = series.shape
    block = rows // BLOCK_SLOTS
    half = width // 2
    head_dim = width // HEADS
    scale = math.log2(math.e) / math.sqrt(head_dim)
    node = lax.axis_index("node")
    me = lax.axis_index("tm")
    core = node % 2
    y_lo = (node // 2) % 2
    x = node // 4
    sibling = node + 1 - 2 * core
    y_peer = node + 2 - 4 * y_lo
    right = ((x + 1) % 4) * 4 + node % 4
    left = ((x + 3) % 4) * 4 + node % 4

    def load(i):
        return pltpu.make_async_copy(operands[i], staged[i], load_sem.at[i])

    for i in range(len(operands)):
        load(i).start()
    barrier = pltpu.get_barrier_semaphore()
    for other in (sibling, y_peer, right, left):
        pl.semaphore_signal(barrier, inc=1, device_id={"node": other}, device_id_type=MESH)

    def greet(k, carry):
        pl.semaphore_signal(
            barrier, inc=1, device_id={"tm": (me + k) % GROUPS}, device_id_type=MESH
        )
        return carry

    lax.fori_loop(1, GROUPS, greet, 0)

    for i in range(4):
        load(i).wait()
    flat = series[...].reshape(window * slab, width)
    for s in range(2):
        cut = pl.ds(s * half, half)
        flat_q[s] = dot(flat, tq[:, cut]).astype(bf16).astype(f32)
        flat_k[s] = dot(flat, tk[:, cut]).astype(bf16).astype(f32)
        flat_v[s] = dot(flat, tv[:, cut]).astype(bf16).astype(f32)
    per = 4
    span = per * window
    row_id = lax.broadcasted_iota(jnp.int32, (span, span), 0)
    col_id = lax.broadcasted_iota(jnp.int32, (span, span), 1)

    def owner(index):
        total = jnp.zeros_like(index)
        for k in range(1, per):
            total = total + (index >= k * window).astype(jnp.int32)
        return total

    seen = (row_id >= col_id) & (owner(row_id) == owner(col_id))
    lane = lax.broadcasted_iota(jnp.int32, (span, width), 1) // head_dim
    half_lane = lax.broadcasted_iota(jnp.int32, (span, half), 1) // head_dim
    ones = jnp.ones((span, half), bf16)
    for g in range(slab // per):
        def gather(ref):
            sides = []
            for s in range(2):
                parts = [
                    ref[s, pl.ds(g * per + i, window, stride=slab), :].astype(bf16)
                    for i in range(per)
                ]
                sides.append(jnp.concatenate(parts, axis=0))
            return jnp.concatenate(sides, axis=1)

        q, k, v = gather(flat_q), gather(flat_k), gather(flat_v)
        for s in range(2):
            values = jnp.concatenate([v[:, s * half : (s + 1) * half], ones], axis=1)
            mixed = jnp.zeros((span, half), f32)
            for i in range(HEADS // 2):
                h = s * (HEADS // 2) + i
                scores = dot_t(jnp.where(lane == h, q, jnp.zeros_like(q)), k)
                scores = jnp.where(seen, scores, -1e30)
                top = jnp.max(scores, axis=1, keepdims=True)
                p = jnp.exp2((scores - top) * scale).astype(bf16)
                a = dot(p, values)
                mixed = jnp.where(half_lane == i, a[:, :half] / a[:, half:], mixed)
            for i in range(per):
                flat_mix[s, pl.ds(g * per + i, window, stride=slab), :] = mixed[
                    i * window : (i + 1) * window
                ]
    for i in range(4, len(operands)):
        load(i).wait()
    mixed = jnp.concatenate([flat_mix[0].astype(bf16), flat_mix[1].astype(bf16)], axis=1)
    first = flat.astype(f32) + dot(mixed, to[...])
    hid[...] = layer_norm(first, gain_first[...]).astype(bf16).reshape(window, slab, width)

    pl.semaphore_wait(barrier, GROUPS - 1 + 4)

    my_rows = pl.ds(pl.multiple_of(me * slab, slab), slab)

    def scatter(t):
        def one(k, carry):
            j = (me + k) % GROUPS
            pltpu.make_async_remote_copy(
                src_ref=hid.at[steps * j + t],
                dst_ref=keys_in.at[t, my_rows, :],
                send_sem=a_send.at[t],
                recv_sem=a_recv.at[t],
                device_id={"tm": j},
                device_id_type=MESH,
            ).start()
            return carry

        lax.fori_loop(1, GROUPS, one, 0)

    for t in range(steps):
        scatter(t)
    for t in range(steps):
        keys_in[t, my_rows, :] = hid[steps * me + t]

    def wait_bytes(ref, sem):
        pltpu.make_async_copy(ref, ref, sem).wait()

    routes = [
        (0, 2, y_peer),
        (0, 3, right),
        (0, 4, left),
        (2, 8, right),
        (2, 9, left),
        (3, 10, right),
        (9, 11, left),
    ]
    shares = [(0, 1, 1), (2, 5, 3), (8, 12, 2), (10, 14, 2)]

    def route(t, i):
        src, dst, other = routes[i]
        return pltpu.make_async_remote_copy(
            src_ref=keys_in.at[t, pl.ds(src * block, block), :],
            dst_ref=keys_in.at[t, pl.ds(dst * block, block), :],
            send_sem=n_send.at[t, i],
            recv_sem=n_recv.at[t, i],
            device_id={"node": other},
            device_id_type=MESH,
        )

    def share(t, i):
        src, dst, count = shares[i]
        return pltpu.make_async_remote_copy(
            src_ref=keys_in.at[t, pl.ds(src * block, count * block), :],
            dst_ref=keys_in.at[t, pl.ds(dst * block, count * block), :],
            send_sem=s_send.at[t, i],
            recv_sem=s_recv.at[t, i],
            device_id={"node": sibling},
            device_id_type=MESH,
        )

    def own_ready(t):
        wait_bytes(keys_in.at[t, pl.ds(0, block - slab), :], a_recv.at[t])
        share(t, 0).start()
        for i in (0, 1, 2):
            route(t, i).start()

    def near_ready(t):
        for i in (0, 1, 2):
            route(t, i).wait_recv()
        for i in (3, 4, 5):
            route(t, i).start()
        share(t, 1).start()

    def side_ready(t):
        for i in (3, 4):
            route(t, i).wait_recv()
        route(t, 6).start()
        share(t, 2).start()

    def far_ready(t):
        for i in (5, 6):
            route(t, i).wait_recv()
        share(t, 3).start()

    def shared(t, i):
        share(t, i).wait_recv()

    chunk = k_buf.shape[1]
    v_buf[:, :, :, half:] = jnp.ones((2, 2, chunk, half), bf16)
    turn = [0]

    def project_queries(t):
        q = (dot(keys_in[t, pl.ds(0, block), :], wq[...]) * scale).astype(bf16)
        lane = lax.broadcasted_iota(jnp.int32, (block, width), 1) // head_dim
        for h in range(HEADS):
            q_mask[t, h] = jnp.where(lane == h, q, jnp.zeros_like(q))

    def attend(t, parts, fresh):
        slot = turn[0] % 2
        turn[0] += 1
        n = 0
        for start, count in parts:
            rows_in = keys_in[t, pl.ds(start * block, count * block), :]
            here = pl.ds(n, count * block)
            k_buf[slot, here, :] = dot(rows_in, wk[...]).astype(bf16)
            v = dot(rows_in, wv[...]).astype(bf16)
            v_buf[slot, 0, here, :half] = v[:, :half]
            v_buf[slot, 1, here, :half] = v[:, half:]
            n += count * block
        for h in range(HEADS):
            s = dot_t(q_mask[t, h], k_buf[slot, :n, :])
            top = jnp.max(s, axis=1, keepdims=True)
            if fresh:
                new = jnp.broadcast_to(top, (block, 128))
            else:
                old = row_max[t, h]
                new = jnp.maximum(old, top)
            p = jnp.exp2(s - wide(new, n // 128)).astype(bf16)
            update = dot(p, v_buf[slot, h // 4, :n, :])
            if fresh:
                acc[t, h] = update
            else:
                fade = jnp.exp2(old - new)
                acc[t, h] = acc[t, h] * wide(fade, width // 128) + update
            row_max[t, h] = new

    def finish(t):
        lane = lax.broadcasted_iota(jnp.int32, (block, half), 1) // head_dim
        sides = []
        for s in range(2):
            mixed = jnp.zeros((block, half), f32)
            for i in range(HEADS // 2):
                a = acc[t, s * (HEADS // 2) + i]
                mixed = jnp.where(lane == i, a[:, :half] / a[:, half:], mixed)
            sides.append(mixed.astype(bf16))
        mixed = jnp.concatenate(sides, axis=1)
        second = keys_in[t, pl.ds(0, block), :].astype(f32) + dot(mixed, wo[...])
        result[t] = layer_norm(second, gain_second[...]).astype(bf16)

    def give(t):
        def one(k, carry):
            j = (me + k) % GROUPS
            pltpu.make_async_remote_copy(
                src_ref=result.at[t, pl.ds(pl.multiple_of(j * slab, slab), slab), :],
                dst_ref=out.at[steps * me + t],
                send_sem=r_send.at[t],
                recv_sem=r_recv.at[t],
                device_id={"tm": j},
                device_id_type=MESH,
            ).start()
            return carry

        lax.fori_loop(1, GROUPS, one, 0)

    own_ready(0)
    project_queries(0)
    shared(0, 0)
    attend(0, [(0, 2)], True)
    near_ready(0)
    own_ready(1)
    attend(0, [(2, 3)], False)
    project_queries(1)
    shared(0, 1)
    attend(0, [(5, 3)], False)
    shared(1, 0)
    attend(1, [(0, 2)], True)
    side_ready(0)
    near_ready(1)
    own_ready(2)
    attend(1, [(2, 3)], False)
    project_queries(2)
    shared(1, 1)
    shared(0, 2)
    attend(1, [(5, 3)], False)
    attend(0, [(8, 2), (12, 2)], False)
    far_ready(0)
    shared(2, 0)
    attend(2, [(0, 2)], True)
    side_ready(1)
    near_ready(2)
    shared(0, 3)
    attend(0, [(10, 2), (14, 2)], False)
    finish(0)
    attend(2, [(2, 3)], False)
    give(0)
    shared(2, 1)
    attend(2, [(5, 3)], False)
    far_ready(1)
    side_ready(2)
    shared(1, 2)
    attend(1, [(8, 2), (12, 2)], False)
    shared(1, 3)
    attend(1, [(10, 2), (14, 2)], False)
    finish(1)
    far_ready(2)
    shared(2, 2)
    attend(2, [(8, 2), (12, 2)], False)
    give(1)
    shared(2, 3)
    attend(2, [(10, 2), (14, 2)], False)
    finish(2)
    give(2)

    def keep(t):
        return pltpu.make_async_copy(
            result.at[t, my_rows, :], out.at[steps * me + t], keep_sem.at[t]
        )

    for t in range(steps):
        keep(t).start()
    for t in range(steps):
        keep(t).wait()
    for t in range(steps):
        wait_bytes(keys_in.at[t, pl.ds(0, block - slab), :], a_send.at[t])
        for i in range(len(routes)):
            route(t, i).wait_send()
        for i in range(len(shares)):
            share(t, i).wait_send()
        wait_bytes(result.at[t, pl.ds(0, block - slab), :], r_send.at[t])
        wait_bytes(result.at[t, pl.ds(0, block - slab), :], r_recv.at[t])


def shards(
    series, t_query, t_key, t_value, t_out, s_query, s_key, s_value, s_out, gain_first, gain_second
):
    window, slab, width = series.shape
    steps = window // GROUPS
    block = slab * GROUPS
    chunk = 4 * block
    hbm = pl.BlockSpec(memory_space=pltpu.HBM)
    weight = pltpu.VMEM((width, width), bf16)
    gain = pltpu.VMEM((1, width), f32)
    flat = pltpu.VMEM((2, window * slab, width // 2), f32)
    return pl.pallas_call(
        block_kernel,
        out_shape=jax.ShapeDtypeStruct(series.shape, bf16),
        in_specs=[hbm] * 11,
        out_specs=hbm,
        scratch_shapes=[
            pltpu.VMEM(series.shape, bf16),
            *[weight] * 8,
            gain,
            gain,
            pltpu.SemaphoreType.DMA((11,)),
            pltpu.SemaphoreType.DMA((steps,)),
            flat,
            flat,
            flat,
            flat,
            pltpu.VMEM((window, slab, width), bf16),
            pltpu.VMEM((steps, BLOCK_SLOTS * block, width), bf16),
            pltpu.VMEM((2, chunk, width), bf16),
            pltpu.VMEM((2, 2, chunk, width), bf16),
            pltpu.VMEM((steps, HEADS, block, width), bf16),
            pltpu.VMEM((steps, HEADS, block, width), f32),
            pltpu.VMEM((steps, HEADS, block, 128), f32),
            pltpu.VMEM((steps, block, width), bf16),
            pltpu.SemaphoreType.DMA((steps,)),
            pltpu.SemaphoreType.DMA((steps,)),
            pltpu.SemaphoreType.DMA((steps, 7)),
            pltpu.SemaphoreType.DMA((steps, 7)),
            pltpu.SemaphoreType.DMA((steps, 4)),
            pltpu.SemaphoreType.DMA((steps, 4)),
            pltpu.SemaphoreType.DMA((steps,)),
            pltpu.SemaphoreType.DMA((steps,)),
        ],
        compiler_params=pltpu.CompilerParams(
            collective_id=0, has_side_effects=True, vmem_limit_bytes=63 * 2**20
        ),
    )(
        series, t_query, t_key, t_value, t_out, s_query, s_key, s_value, s_out,
        gain_first.reshape(1, width), gain_second.reshape(1, width),
    )


def solution(mesh):
    in_specs = (P(None, ("node", "tm"), None), P(), P(), P(), P(), P(), P(), P(), P(), P(), P())
    out_specs = P(None, ("node", "tm"), None)
    return jax.shard_map(shards, mesh=mesh, in_specs=in_specs, out_specs=out_specs, check_vma=False)
```

```python
import math

import jax
import jax.numpy as jnp
from jax import lax
from jax.experimental import pallas as pl
from jax.experimental.pallas import tpu as pltpu
from jax.sharding import PartitionSpec as P

HEADS = 8
epsilon = 1e-05
f32, bf16 = jnp.float32, jnp.bfloat16
MESH = pl.DeviceIdType.MESH
GROUPS = 16
BLOCK_SLOTS = 16


def layer_norm(values, gain):
    center = values - jnp.mean(values, axis=-1, keepdims=True)
    spread = jnp.mean(center * center, axis=-1, keepdims=True)
    return center * lax.rsqrt(spread + epsilon) * gain


def dot_t(a, b):
    return lax.dot_general(a, b, (((1,), (1,)), ((), ())), preferred_element_type=f32)


def dot(a, b):
    return jnp.dot(a, b, preferred_element_type=f32)


def wide(column, count):
    return jnp.concatenate([column] * count, axis=1)


def block_kernel(
    *refs,
):
    operands, refs = refs[:11], refs[11:]
    staged, refs = refs[1:12], (refs[0],) + refs[12:]
    body(operands, staged, *refs)


def body(
    operands, staged, out, load_sem, keep_sem,
    flat_q, flat_k, flat_v, flat_mix, hid,
    keys_in, k_buf, v_buf, q_mask, acc, row_max, result,
    a_send, a_recv, n_send, n_recv, s_send, s_recv, r_send, r_recv,
):
    series, tq, tk, tv, to, wq, wk, wv, wo, gain_first, gain_second = staged
    steps, rows, width = keys_in.shape
    window, slab, _ = series.shape
    block = rows // BLOCK_SLOTS
    half = width // 2
    head_dim = width // HEADS
    scale = math.log2(math.e) / math.sqrt(head_dim)
    node = lax.axis_index("node")
    me = lax.axis_index("tm")
    core = node % 2
    y_lo = (node // 2) % 2
    x = node // 4
    sibling = node + 1 - 2 * core
    y_peer = node + 2 - 4 * y_lo
    right = ((x + 1) % 4) * 4 + node % 4
    left = ((x + 3) % 4) * 4 + node % 4

    def load(i):
        return pltpu.make_async_copy(operands[i], staged[i], load_sem.at[i])

    for i in range(len(operands)):
        load(i).start()
    barrier = pltpu.get_barrier_semaphore()
    for other in (sibling, y_peer, right, left):
        pl.semaphore_signal(barrier, inc=1, device_id={"node": other}, device_id_type=MESH)

    def greet(k, carry):
        pl.semaphore_signal(
            barrier, inc=1, device_id={"tm": (me + k) % GROUPS}, device_id_type=MESH
        )
        return carry

    lax.fori_loop(1, GROUPS, greet, 0)

    for i in range(4):
        load(i).wait()
    flat = series[...].reshape(window * slab, width)
    for s in range(2):
        cut = pl.ds(s * half, half)
        flat_q[s] = dot(flat, tq[:, cut]).astype(bf16).astype(f32)
        flat_k[s] = dot(flat, tk[:, cut]).astype(bf16).astype(f32)
        flat_v[s] = dot(flat, tv[:, cut]).astype(bf16).astype(f32)
    per = 4
    span = per * window
    row_id = lax.broadcasted_iota(jnp.int32, (span, span), 0)
    col_id = lax.broadcasted_iota(jnp.int32, (span, span), 1)

    def owner(index):
        total = jnp.zeros_like(index)
        for k in range(1, per):
            total = total + (index >= k * window).astype(jnp.int32)
        return total

    seen = (row_id >= col_id) & (owner(row_id) == owner(col_id))
    lane = lax.broadcasted_iota(jnp.int32, (span, width), 1) // head_dim
    half_lane = lax.broadcasted_iota(jnp.int32, (span, half), 1) // head_dim
    ones = jnp.ones((span, half), bf16)
    for g in range(slab // per):
        def gather(ref):
            sides = []
            for s in range(2):
                parts = [
                    ref[s, pl.ds(g * per + i, window, stride=slab), :].astype(bf16)
                    for i in range(per)
                ]
                sides.append(jnp.concatenate(parts, axis=0))
            return jnp.concatenate(sides, axis=1)

        q, k, v = gather(flat_q), gather(flat_k), gather(flat_v)
        for s in range(2):
            values = jnp.concatenate([v[:, s * half : (s + 1) * half], ones], axis=1)
            mixed = jnp.zeros((span, half), f32)
            for i in range(HEADS // 2):
                h = s * (HEADS // 2) + i
                scores = dot_t(jnp.where(lane == h, q, jnp.zeros_like(q)), k)
                scores = jnp.where(seen, scores, -1e30)
                top = jnp.max(scores, axis=1, keepdims=True)
                p = jnp.exp2((scores - top) * scale).astype(bf16)
                a = dot(p, values)
                mixed = jnp.where(half_lane == i, a[:, :half] / a[:, half:], mixed)
            for i in range(per):
                flat_mix[s, pl.ds(g * per + i, window, stride=slab), :] = mixed[
                    i * window : (i + 1) * window
                ]
    for i in range(4, len(operands)):
        load(i).wait()
    mixed = jnp.concatenate([flat_mix[0].astype(bf16), flat_mix[1].astype(bf16)], axis=1)
    first = flat.astype(f32) + dot(mixed, to[...])
    hid[...] = layer_norm(first, gain_first[...]).astype(bf16).reshape(window, slab, width)

    pl.semaphore_wait(barrier, GROUPS - 1 + 4)

    my_rows = pl.ds(pl.multiple_of(me * slab, slab), slab)

    def scatter(t):
        def one(k, carry):
            j = (me + k) % GROUPS
            pltpu.make_async_remote_copy(
                src_ref=hid.at[steps * j + t],
                dst_ref=keys_in.at[t, my_rows, :],
                send_sem=a_send.at[t],
                recv_sem=a_recv.at[t],
                device_id={"tm": j},
                device_id_type=MESH,
            ).start()
            return carry

        lax.fori_loop(1, GROUPS, one, 0)

    for t in range(steps):
        scatter(t)
    for t in range(steps):
        keys_in[t, my_rows, :] = hid[steps * me + t]

    def wait_bytes(ref, sem):
        pltpu.make_async_copy(ref, ref, sem).wait()

    cut = block // 2
    routes = [
        (0, 2 * block, block, y_peer),
        (0, 3 * block, block, right),
        (0, 4 * block, block, left),
        (2 * block, 8 * block, block, right),
        (2 * block, 9 * block, block, left),
        (3 * block, 10 * block, cut, right),
        (4 * block + cut, 10 * block + cut, cut, left),
        (8 * block, 11 * block, cut, right),
        (9 * block + cut, 11 * block + cut, cut, left),
    ]
    shares = [(0, 1, 1), (2, 5, 3), (8, 12, 2), (10, 14, 2)]

    def route(t, i):
        src, dst, count, other = routes[i]
        return pltpu.make_async_remote_copy(
            src_ref=keys_in.at[t, pl.ds(src, count), :],
            dst_ref=keys_in.at[t, pl.ds(dst, count), :],
            send_sem=n_send.at[t, i],
            recv_sem=n_recv.at[t, i],
            device_id={"node": other},
            device_id_type=MESH,
        )

    def share(t, i):
        src, dst, count = shares[i]
        return pltpu.make_async_remote_copy(
            src_ref=keys_in.at[t, pl.ds(src * block, count * block), :],
            dst_ref=keys_in.at[t, pl.ds(dst * block, count * block), :],
            send_sem=s_send.at[t, i],
            recv_sem=s_recv.at[t, i],
            device_id={"node": sibling},
            device_id_type=MESH,
        )

    def own_ready(t):
        wait_bytes(keys_in.at[t, pl.ds(0, block - slab), :], a_recv.at[t])
        share(t, 0).start()
        for i in (1, 2, 0):
            route(t, i).start()

    def near_ready(t):
        for i in (0, 1, 2):
            route(t, i).wait_recv()
        for i in (3, 4, 5, 6):
            route(t, i).start()
        share(t, 1).start()

    def side_ready(t):
        for i in (3, 4):
            route(t, i).wait_recv()
        route(t, 7).start()
        route(t, 8).start()
        share(t, 2).start()

    def far_ready(t):
        for i in (5, 6, 7, 8):
            route(t, i).wait_recv()
        share(t, 3).start()

    def shared(t, i):
        share(t, i).wait_recv()

    chunk = k_buf.shape[1]
    v_buf[:, :, :, half:] = jnp.ones((2, 2, chunk, half), bf16)
    turn = [0]

    def project_queries(t):
        q = (dot(keys_in[t, pl.ds(0, block), :], wq[...]) * scale).astype(bf16)
        lane = lax.broadcasted_iota(jnp.int32, (block, width), 1) // head_dim
        for h in range(HEADS):
            q_mask[t, h] = jnp.where(lane == h, q, jnp.zeros_like(q))

    def attend(t, parts, fresh):
        slot = turn[0] % 2
        turn[0] += 1
        n = 0
        for start, count in parts:
            first_row = pl.multiple_of(start * block, block)
            rows_in = keys_in[t, pl.ds(first_row, count * block), :]
            here = pl.ds(n, count * block)
            k_buf[slot, here, :] = dot(rows_in, wk[...]).astype(bf16)
            v = dot(rows_in, wv[...]).astype(bf16)
            v_buf[slot, 0, here, :half] = v[:, :half]
            v_buf[slot, 1, here, :half] = v[:, half:]
            n += count * block
        for h in range(HEADS):
            s = dot_t(q_mask[t, h], k_buf[slot, :n, :])
            top = jnp.max(s, axis=1, keepdims=True)
            if fresh:
                new = jnp.broadcast_to(top, (block, 128))
            else:
                old = row_max[t, h]
                new = jnp.maximum(old, top)
            p = jnp.exp2(s - wide(new, n // 128)).astype(bf16)
            update = dot(p, v_buf[slot, h // 4, :n, :])
            if fresh:
                acc[t, h] = update
            else:
                fade = jnp.exp2(old - new)
                acc[t, h] = acc[t, h] * wide(fade, width // 128) + update
            row_max[t, h] = new

    def finish(t):
        lane = lax.broadcasted_iota(jnp.int32, (block, half), 1) // head_dim
        sides = []
        for s in range(2):
            mixed = jnp.zeros((block, half), f32)
            for i in range(HEADS // 2):
                a = acc[t, s * (HEADS // 2) + i]
                mixed = jnp.where(lane == i, a[:, :half] / a[:, half:], mixed)
            sides.append(mixed.astype(bf16))
        mixed = jnp.concatenate(sides, axis=1)
        second = keys_in[t, pl.ds(0, block), :].astype(f32) + dot(mixed, wo[...])
        result[t] = layer_norm(second, gain_second[...]).astype(bf16)

    def give(t):
        def one(k, carry):
            j = (me + k) % GROUPS
            pltpu.make_async_remote_copy(
                src_ref=result.at[t, pl.ds(pl.multiple_of(j * slab, slab), slab), :],
                dst_ref=out.at[steps * me + t],
                send_sem=r_send.at[t],
                recv_sem=r_recv.at[t],
                device_id={"tm": j},
                device_id_type=MESH,
            ).start()
            return carry

        lax.fori_loop(1, GROUPS, one, 0)

    def near(t):
        def one(i, carry):
            pl.when(i == 1)(lambda: shared(t, 1))
            attend(t, [(2 + 3 * i, 3)], False)
            return carry

        lax.fori_loop(0, 2, one, 0)

    def far(t, between):
        def one(i, carry):
            pl.when(i == 1)(between)
            attend(t, [(8 + 2 * i, 2), (12 + 2 * i, 2)], False)
            return carry

        lax.fori_loop(0, 2, one, 0)

    def turn_last():
        give(1)
        shared(2, 3)

    own_ready(0)
    own_ready(1)
    project_queries(0)
    shared(0, 0)
    attend(0, [(0, 2)], True)
    near_ready(0)
    own_ready(2)
    project_queries(1)
    near(0)
    shared(1, 0)
    attend(1, [(0, 2)], True)
    side_ready(0)
    near_ready(1)
    project_queries(2)
    near(1)
    shared(0, 2)
    attend(0, [(8, 2), (12, 2)], False)
    far_ready(0)
    shared(2, 0)
    attend(2, [(0, 2)], True)
    side_ready(1)
    near_ready(2)
    shared(0, 3)
    attend(0, [(10, 2), (14, 2)], False)
    finish(0)
    give(0)
    near(2)
    far_ready(1)
    side_ready(2)
    shared(1, 2)
    far(1, lambda: shared(1, 3))
    finish(1)
    far_ready(2)
    shared(2, 2)
    far(2, turn_last)
    finish(2)
    give(2)

    def keep(t):
        return pltpu.make_async_copy(
            result.at[t, my_rows, :], out.at[steps * me + t], keep_sem.at[t]
        )

    for t in range(steps):
        keep(t).start()
    for t in range(steps):
        keep(t).wait()
    for t in range(steps):
        wait_bytes(keys_in.at[t, pl.ds(0, block - slab), :], a_send.at[t])
        for i in range(len(routes)):
            route(t, i).wait_send()
        for i in range(len(shares)):
            share(t, i).wait_send()
        wait_bytes(result.at[t, pl.ds(0, block - slab), :], r_send.at[t])
        wait_bytes(result.at[t, pl.ds(0, block - slab), :], r_recv.at[t])


def shards(
    series, t_query, t_key, t_value, t_out, s_query, s_key, s_value, s_out, gain_first, gain_second
):
    window, slab, width = series.shape
    steps = window // GROUPS
    block = slab * GROUPS
    chunk = 4 * block
    hbm = pl.BlockSpec(memory_space=pltpu.HBM)
    weight = pltpu.VMEM((width, width), bf16)
    gain = pltpu.VMEM((1, width), f32)
    flat = pltpu.VMEM((2, window * slab, width // 2), f32)
    return pl.pallas_call(
        block_kernel,
        out_shape=jax.ShapeDtypeStruct(series.shape, bf16),
        in_specs=[hbm] * 11,
        out_specs=hbm,
        scratch_shapes=[
            pltpu.VMEM(series.shape, bf16),
            *[weight] * 8,
            gain,
            gain,
            pltpu.SemaphoreType.DMA((11,)),
            pltpu.SemaphoreType.DMA((steps,)),
            flat,
            flat,
            flat,
            flat,
            pltpu.VMEM((window, slab, width), bf16),
            pltpu.VMEM((steps, BLOCK_SLOTS * block, width), bf16),
            pltpu.VMEM((2, chunk, width), bf16),
            pltpu.VMEM((2, 2, chunk, width), bf16),
            pltpu.VMEM((steps, HEADS, block, width), bf16),
            pltpu.VMEM((steps, HEADS, block, width), f32),
            pltpu.VMEM((steps, HEADS, block, 128), f32),
            pltpu.VMEM((steps, block, width), bf16),
            pltpu.SemaphoreType.DMA((steps,)),
            pltpu.SemaphoreType.DMA((steps,)),
            pltpu.SemaphoreType.DMA((steps, 9)),
            pltpu.SemaphoreType.DMA((steps, 9)),
            pltpu.SemaphoreType.DMA((steps, 4)),
            pltpu.SemaphoreType.DMA((steps, 4)),
            pltpu.SemaphoreType.DMA((steps,)),
            pltpu.SemaphoreType.DMA((steps,)),
        ],
        compiler_params=pltpu.CompilerParams(
            collective_id=0, has_side_effects=True, vmem_limit_bytes=63 * 2**20
        ),
    )(
        series, t_query, t_key, t_value, t_out, s_query, s_key, s_value, s_out,
        gain_first.reshape(1, width), gain_second.reshape(1, width),
    )


def solution(mesh):
    in_specs = (P(None, ("node", "tm"), None), P(), P(), P(), P(), P(), P(), P(), P(), P(), P())
    out_specs = P(None, ("node", "tm"), None)
    return jax.shard_map(shards, mesh=mesh, in_specs=in_specs, out_specs=out_specs, check_vma=False)
```

```python
import math

import jax
import jax.numpy as jnp
from jax import lax
from jax.experimental import pallas as pl
from jax.experimental.pallas import tpu as pltpu
from jax.sharding import PartitionSpec as P

HEADS = 8
epsilon = 1e-05
f32, bf16 = jnp.float32, jnp.bfloat16
MESH = pl.DeviceIdType.MESH
GROUPS = 16
BLOCK_SLOTS = 16


def layer_norm(values, gain):
    center = values - jnp.mean(values, axis=-1, keepdims=True)
    spread = jnp.mean(center * center, axis=-1, keepdims=True)
    return center * lax.rsqrt(spread + epsilon) * gain


def dot_t(a, b):
    return lax.dot_general(a, b, (((1,), (1,)), ((), ())), preferred_element_type=f32)


def dot(a, b):
    return jnp.dot(a, b, preferred_element_type=f32)


def wide(column, count):
    return jnp.concatenate([column] * count, axis=1)


def block_kernel(
    *refs,
):
    operands, refs = refs[:11], refs[11:]
    staged, refs = refs[1:12], (refs[0],) + refs[12:]
    body(operands, staged, *refs)


def body(
    operands, staged, out, load_sem, keep_sem,
    flat_q, flat_k, flat_v, flat_mix, hid,
    keys_in, v_buf, q_mask, acc, row_max, result,
    a_send, a_recv, n_send, n_recv, s_send, s_recv, r_send, r_recv,
):
    series, tq, tk, tv, to, wq, wk, wv, wo, gain_first, gain_second = staged
    steps, rows, width = keys_in.shape
    window, slab, _ = series.shape
    block = rows // BLOCK_SLOTS
    half = width // 2
    head_dim = width // HEADS
    scale = math.log2(math.e) / math.sqrt(head_dim)
    node = lax.axis_index("node")
    me = lax.axis_index("tm")
    core = node % 2
    y_lo = (node // 2) % 2
    x = node // 4
    sibling = node + 1 - 2 * core
    y_peer = node + 2 - 4 * y_lo
    right = ((x + 1) % 4) * 4 + node % 4
    left = ((x + 3) % 4) * 4 + node % 4

    def load(i):
        return pltpu.make_async_copy(operands[i], staged[i], load_sem.at[i])

    for i in range(len(operands)):
        load(i).start()
    barrier = pltpu.get_barrier_semaphore()
    for other in (sibling, y_peer, right, left):
        pl.semaphore_signal(barrier, inc=1, device_id={"node": other}, device_id_type=MESH)

    def greet(k, carry):
        pl.semaphore_signal(
            barrier, inc=1, device_id={"tm": (me + k) % GROUPS}, device_id_type=MESH
        )
        return carry

    lax.fori_loop(1, GROUPS, greet, 0)

    for i in range(4):
        load(i).wait()
    flat = series[...].reshape(window * slab, width)
    for s in range(2):
        cut = pl.ds(s * half, half)
        flat_q[s] = dot(flat, tq[:, cut]).astype(bf16).astype(f32)
        flat_k[s] = dot(flat, tk[:, cut]).astype(bf16).astype(f32)
        flat_v[s] = dot(flat, tv[:, cut]).astype(bf16).astype(f32)
    per = 4
    span = per * window
    row_id = lax.broadcasted_iota(jnp.int32, (span, span), 0)
    col_id = lax.broadcasted_iota(jnp.int32, (span, span), 1)

    def owner(index):
        total = jnp.zeros_like(index)
        for k in range(1, per):
            total = total + (index >= k * window).astype(jnp.int32)
        return total

    seen = (row_id >= col_id) & (owner(row_id) == owner(col_id))
    lane = lax.broadcasted_iota(jnp.int32, (span, width), 1) // head_dim
    half_lane = lax.broadcasted_iota(jnp.int32, (span, half), 1) // head_dim
    ones = jnp.ones((span, half), bf16)
    for g in range(slab // per):
        def gather(ref):
            sides = []
            for s in range(2):
                parts = [
                    ref[s, pl.ds(g * per + i, window, stride=slab), :].astype(bf16)
                    for i in range(per)
                ]
                sides.append(jnp.concatenate(parts, axis=0))
            return jnp.concatenate(sides, axis=1)

        q, k, v = gather(flat_q), gather(flat_k), gather(flat_v)
        for s in range(2):
            values = jnp.concatenate([v[:, s * half : (s + 1) * half], ones], axis=1)
            mixed = jnp.zeros((span, half), f32)
            for i in range(HEADS // 2):
                h = s * (HEADS // 2) + i
                scores = dot_t(jnp.where(lane == h, q, jnp.zeros_like(q)), k)
                scores = jnp.where(seen, scores, -1e30)
                top = jnp.max(scores, axis=1, keepdims=True)
                p = jnp.exp2((scores - top) * scale).astype(bf16)
                a = dot(p, values)
                mixed = jnp.where(half_lane == i, a[:, :half] / a[:, half:], mixed)
            for i in range(per):
                flat_mix[s, pl.ds(g * per + i, window, stride=slab), :] = mixed[
                    i * window : (i + 1) * window
                ]
    for i in range(4, len(operands)):
        load(i).wait()
    mixed = jnp.concatenate([flat_mix[0].astype(bf16), flat_mix[1].astype(bf16)], axis=1)
    first = flat.astype(f32) + dot(mixed, to[...])
    hid[...] = layer_norm(first, gain_first[...]).astype(bf16).reshape(window, slab, width)

    pl.semaphore_wait(barrier, GROUPS - 1 + 4)

    far_first = (4, 12, 3, 13, 5, 11, 2, 14, 6, 10, 1, 15, 7, 9, 8)
    my_rows = pl.ds(pl.multiple_of(me * slab, slab), slab)

    def scatter(t):
        def one(k, carry):
            j = (me + k) % GROUPS
            pltpu.make_async_remote_copy(
                src_ref=hid.at[steps * j + t],
                dst_ref=keys_in.at[t, my_rows, :],
                send_sem=a_send.at[t],
                recv_sem=a_recv.at[t],
                device_id={"tm": j},
                device_id_type=MESH,
            ).start()
            return carry

        for k in far_first:
            one(k, 0)

    for t in range(steps):
        scatter(t)
    for t in range(steps):
        keys_in[t, my_rows, :] = hid[steps * me + t]

    def wait_bytes(ref, sem):
        pltpu.make_async_copy(ref, ref, sem).wait()

    cut = block // 2
    routes = [
        (0, 2 * block, block, y_peer),
        (0, 3 * block, block, right),
        (0, 4 * block, block, left),
        (2 * block, 8 * block, block, right),
        (2 * block, 9 * block, block, left),
        (3 * block, 10 * block, cut, right),
        (4 * block + cut, 10 * block + cut, cut, left),
        (8 * block, 11 * block, cut, right),
        (9 * block + cut, 11 * block + cut, cut, left),
    ]
    shares = [(0, 1, 1), (2, 5, 3), (8, 12, 2), (10, 14, 2)]

    def route(t, i):
        src, dst, count, other = routes[i]
        return pltpu.make_async_remote_copy(
            src_ref=keys_in.at[t, pl.ds(src, count), :],
            dst_ref=keys_in.at[t, pl.ds(dst, count), :],
            send_sem=n_send.at[t, i],
            recv_sem=n_recv.at[t, i],
            device_id={"node": other},
            device_id_type=MESH,
        )

    def share(t, i):
        src, dst, count = shares[i]
        return pltpu.make_async_remote_copy(
            src_ref=keys_in.at[t, pl.ds(src * block, count * block), :],
            dst_ref=keys_in.at[t, pl.ds(dst * block, count * block), :],
            send_sem=s_send.at[t, i],
            recv_sem=s_recv.at[t, i],
            device_id={"node": sibling},
            device_id_type=MESH,
        )

    def own_ready(t):
        wait_bytes(keys_in.at[t, pl.ds(0, block - slab), :], a_recv.at[t])
        share(t, 0).start()
        for i in (1, 2, 0):
            route(t, i).start()

    def near_ready(t):
        for i in (0, 1, 2):
            route(t, i).wait_recv()
        for i in (3, 4, 5, 6):
            route(t, i).start()
        share(t, 1).start()

    def side_ready(t):
        for i in (3, 4):
            route(t, i).wait_recv()
        route(t, 7).start()
        route(t, 8).start()
        share(t, 2).start()

    def far_ready(t):
        for i in (5, 6, 7, 8):
            route(t, i).wait_recv()
        share(t, 3).start()

    def shared(t, i):
        share(t, i).wait_recv()

    chunk = v_buf.shape[2]
    v_buf[:, :, :, half:] = jnp.ones((2, 2, chunk, half), bf16)
    turn = [0]

    def project_queries(t):
        q = (dot(keys_in[t, pl.ds(0, block), :], wq[...]) * scale).astype(bf16)
        lane = lax.broadcasted_iota(jnp.int32, (block, width), 1) // head_dim
        for h in range(HEADS):
            q_mask[t, h] = dot_t(jnp.where(lane == h, q, jnp.zeros_like(q)), wk[...]).astype(bf16)

    def attend(t, parts, fresh):
        slot = turn[0] % 2
        turn[0] += 1
        n = 0
        cuts = []
        for start, count in parts:
            first_row = pl.multiple_of(start * block, block)
            rows_in = keys_in[t, pl.ds(first_row, count * block), :]
            here = pl.ds(n, count * block)
            cuts.append((first_row, count * block))
            v = dot(rows_in, wv[...]).astype(bf16)
            v_buf[slot, 0, here, :half] = v[:, :half]
            v_buf[slot, 1, here, :half] = v[:, half:]
            n += count * block
        for h in range(HEADS):
            s = [dot_t(q_mask[t, h], keys_in[t, pl.ds(a, size), :]) for a, size in cuts]
            s = s[0] if len(s) == 1 else jnp.concatenate(s, axis=1)
            top = jnp.max(s, axis=1, keepdims=True)
            if fresh:
                new = jnp.broadcast_to(top, (block, 128))
            else:
                old = row_max[t, h]
                new = jnp.maximum(old, top)
            p = jnp.exp2(s - wide(new, n // 128)).astype(bf16)
            update = dot(p, v_buf[slot, h // 4, :n, :])
            if fresh:
                acc[t, h] = update
            else:
                fade = jnp.exp2(old - new)
                acc[t, h] = acc[t, h] * wide(fade, width // 128) + update
            row_max[t, h] = new

    def finish(t):
        lane = lax.broadcasted_iota(jnp.int32, (block, half), 1) // head_dim
        sides = []
        for s in range(2):
            mixed = jnp.zeros((block, half), f32)
            for i in range(HEADS // 2):
                a = acc[t, s * (HEADS // 2) + i]
                mixed = jnp.where(lane == i, a[:, :half] / a[:, half:], mixed)
            sides.append(mixed.astype(bf16))
        mixed = jnp.concatenate(sides, axis=1)
        second = keys_in[t, pl.ds(0, block), :].astype(f32) + dot(mixed, wo[...])
        result[t] = layer_norm(second, gain_second[...]).astype(bf16)

    def give(t):
        def one(k, carry):
            j = (me + k) % GROUPS
            pltpu.make_async_remote_copy(
                src_ref=result.at[t, pl.ds(pl.multiple_of(j * slab, slab), slab), :],
                dst_ref=out.at[steps * me + t],
                send_sem=r_send.at[t],
                recv_sem=r_recv.at[t],
                device_id={"tm": j},
                device_id_type=MESH,
            ).start()
            return carry

        for k in far_first:
            one(k, 0)

    def near(t):
        def one(i, carry):
            pl.when(i == 1)(lambda: shared(t, 1))
            attend(t, [(2 + 3 * i, 3)], False)
            return carry

        lax.fori_loop(0, 2, one, 0)

    def far(t, between):
        def one(i, carry):
            pl.when(i == 1)(between)
            attend(t, [(8 + 2 * i, 2), (12 + 2 * i, 2)], False)
            return carry

        lax.fori_loop(0, 2, one, 0)

    def turn_last():
        give(1)
        shared(2, 3)

    own_ready(0)
    own_ready(1)
    project_queries(0)
    shared(0, 0)
    attend(0, [(0, 2)], True)
    project_queries(1)
    shared(1, 0)
    attend(1, [(0, 2)], True)
    near_ready(0)
    own_ready(2)
    near(0)
    side_ready(0)
    near_ready(1)
    project_queries(2)
    near(1)
    shared(0, 2)
    attend(0, [(8, 2), (12, 2)], False)
    far_ready(0)
    shared(2, 0)
    attend(2, [(0, 2)], True)
    side_ready(1)
    near_ready(2)
    shared(0, 3)
    attend(0, [(10, 2), (14, 2)], False)
    finish(0)
    give(0)
    near(2)
    far_ready(1)
    side_ready(2)
    shared(1, 2)
    far(1, lambda: shared(1, 3))
    finish(1)
    far_ready(2)
    shared(2, 2)
    far(2, turn_last)
    finish(2)
    give(2)

    def keep(t):
        return pltpu.make_async_copy(
            result.at[t, my_rows, :], out.at[steps * me + t], keep_sem.at[t]
        )

    for t in range(steps):
        keep(t).start()
    for t in range(steps):
        keep(t).wait()
    for t in range(steps):
        wait_bytes(keys_in.at[t, pl.ds(0, block - slab), :], a_send.at[t])
        for i in range(len(routes)):
            route(t, i).wait_send()
        for i in range(len(shares)):
            share(t, i).wait_send()
        wait_bytes(result.at[t, pl.ds(0, block - slab), :], r_send.at[t])
        wait_bytes(result.at[t, pl.ds(0, block - slab), :], r_recv.at[t])


def shards(
    series, t_query, t_key, t_value, t_out, s_query, s_key, s_value, s_out, gain_first, gain_second
):
    window, slab, width = series.shape
    steps = window // GROUPS
    block = slab * GROUPS
    chunk = 4 * block
    hbm = pl.BlockSpec(memory_space=pltpu.HBM)
    weight = pltpu.VMEM((width, width), bf16)
    gain = pltpu.VMEM((1, width), f32)
    flat = pltpu.VMEM((2, window * slab, width // 2), f32)
    return pl.pallas_call(
        block_kernel,
        out_shape=jax.ShapeDtypeStruct(series.shape, bf16),
        in_specs=[hbm] * 11,
        out_specs=hbm,
        scratch_shapes=[
            pltpu.VMEM(series.shape, bf16),
            *[weight] * 8,
            gain,
            gain,
            pltpu.SemaphoreType.DMA((11,)),
            pltpu.SemaphoreType.DMA((steps,)),
            flat,
            flat,
            flat,
            flat,
            pltpu.VMEM((window, slab, width), bf16),
            pltpu.VMEM((steps, BLOCK_SLOTS * block, width), bf16),
            pltpu.VMEM((2, 2, chunk, width), bf16),
            pltpu.VMEM((steps, HEADS, block, width), bf16),
            pltpu.VMEM((steps, HEADS, block, width), f32),
            pltpu.VMEM((steps, HEADS, block, 128), f32),
            pltpu.VMEM((steps, block, width), bf16),
            pltpu.SemaphoreType.DMA((steps,)),
            pltpu.SemaphoreType.DMA((steps,)),
            pltpu.SemaphoreType.DMA((steps, 9)),
            pltpu.SemaphoreType.DMA((steps, 9)),
            pltpu.SemaphoreType.DMA((steps, 4)),
            pltpu.SemaphoreType.DMA((steps, 4)),
            pltpu.SemaphoreType.DMA((steps,)),
            pltpu.SemaphoreType.DMA((steps,)),
        ],
        compiler_params=pltpu.CompilerParams(
            collective_id=0, has_side_effects=True, vmem_limit_bytes=63 * 2**20
        ),
    )(
        series, t_query, t_key, t_value, t_out, s_query, s_key, s_value, s_out,
        gain_first.reshape(1, width), gain_second.reshape(1, width),
    )


def solution(mesh):
    in_specs = (P(None, ("node", "tm"), None), P(), P(), P(), P(), P(), P(), P(), P(), P(), P())
    out_specs = P(None, ("node", "tm"), None)
    return jax.shard_map(shards, mesh=mesh, in_specs=in_specs, out_specs=out_specs, check_vma=False)
```
